32 devices in a mesh: group: 2 (over y), chan: 4 (over x, core), tm: 4 (over z).
Axes of the slice: x: 2, y: 2, z: 4, core: 2. Of those that a mesh axis runs over, the one named last changes fastest.
Arguments:
- voltages: bfloat16 [2, 32, 1024, 1024], P(None, ('group', 'tm'), 'chan'), parts along dimension 1, may hold values from -6 to 6
- feed_position: int32 [1024, 2], replicated, may hold values from 0 to 63
- beam_steering: int32 [256, 2], P('group'), parts along dimension 0, may hold values from 0 to 63
- synthesis_taps: float32 [4, 1024], replicated, may hold values from 0.2 to 1
Outputs:
- synthesized: bfloat16 [2, 128, 32, 1024], P(None, 'chan', ('group', 'tm')), parts along dimension 2
The draws below stay inside these ranges and needn't reach their ends.
There are 2 independent parts, one for each index of `group`. The reference program is written for one: setup_inputs(seed, part) draws one part's arguments, and reference() takes and returns one part's arrays. A program takes and returns all parts, laid end to end along the dimension named above; an argument that names none is the same for every part. Nothing has to cross between parts.
All inputs are finite; a program needn't handle non-finite values.
Results may differ from the reference program's by a relative error of at most 0.0085.
Values may be sent and summed in bfloat16 or wider, within the bound.
A program may use at most 64 MiB of HBM per device.

```python
import math
import jax
import jax.numpy as jnp
from jax import lax

F = 1024
C = 1024
BEAMS = 128
TAPS = 4
PHASES = 4096
FRAMES = 16


def touch_ends(drawn, stream_key, smallest, top_value):
    spot = [jax.random.randint(jax.random.fold_in(stream_key, axis), (), 0, length) for axis, length in enumerate(drawn.shape)]
    main_axis = drawn.shape.index(max(drawn.shape))
    beside = spot[:main_axis] + [(spot[main_axis] + 1) % drawn.shape[main_axis]] + spot[main_axis + 1:]
    return drawn.at[tuple(spot)].set(smallest).at[tuple(beside)].set(top_value)


def block_levels(rng, shape, cuts, least, top_value):
    level, own = 1.0, jax.random.fold_in(rng, 6)
    for axis_at, blocks in cuts:
        draws = jnp.exp(jax.random.uniform(jax.random.fold_in(own, axis_at), (blocks,), jnp.float32, least / len(cuts), top_value / len(cuts)))
        level = level * jnp.repeat(draws, shape[axis_at] // blocks).reshape([-1 if axis == axis_at else 1 for axis in range(len(shape))])
    return level


def gaussian(rng, dims, deviation, most, cuts=(), kind=jnp.bfloat16):
    entries = deviation * jax.random.normal(rng, dims, jnp.float32)
    if cuts:
        entries = entries * block_levels(rng, dims, cuts, -0.22, 0.18)
    return jnp.clip(entries, -most, most).astype(kind)


def setup_inputs(seed: int = 0, part: int = 0) -> dict:
    key_of = jax.random.split(jax.random.key(seed), 5)
    part_splits = jax.random.split(jax.random.fold_in(key_of[4], part), 5)
    return {
        "voltages": gaussian(part_splits[0], (2, FRAMES, F, C), 1.0, 6.0, ((1, 4), (2, 4))),
        "feed_position": touch_ends(jax.random.randint(key_of[1], (F, 2), 0, 64), jax.random.fold_in(key_of[1], 1), 0, 63).astype(jnp.int32),
        "beam_steering": touch_ends(jax.random.randint(part_splits[2], (BEAMS, 2), 0, 64), jax.random.fold_in(part_splits[2], 1), 0, 63).astype(jnp.int32),
        "synthesis_taps": jnp.clip(jax.random.uniform(key_of[3], (TAPS, C), jnp.float32, 0.2, 1.0), 0.2, 1.0),
    }


def compute_delays(feed_position, beam_steering):
    first = feed_position[:, 0:1] * beam_steering[:, 0][None, :]
    second = feed_position[:, 1:2] * beam_steering[:, 1][None, :]
    return (first + second) % PHASES

def make_weights(delays, channel_ids):
    phases = channel_ids[:, None, None] * delays[None, :, :] % PHASES
    angles = phases.astype(jnp.float32) * (2.0 * math.pi / PHASES)
    return jnp.concatenate([jnp.cos(angles), jnp.sin(angles)], axis=-1).astype(jnp.bfloat16)

def combine(product):
    half = product.shape[-1] // 2
    real_part = product[0, ..., :half] - product[1, ..., half:]
    imag_part = product[0, ..., half:] + product[1, ..., :half]
    return (jnp.stack([real_part, imag_part]) * (1.0 / math.sqrt(F))).astype(jnp.bfloat16)

def make_basis():
    rows = jnp.arange(C, dtype=jnp.int32)
    products = rows[:, None] * rows[None, :] % C
    angles = products.astype(jnp.float32) * (2.0 * math.pi / C)
    cosine = jnp.cos(angles)
    sine = jnp.sin(angles)
    upper = jnp.concatenate([cosine, sine], axis=1)
    lower = jnp.concatenate([-sine, cosine], axis=1)
    return jnp.stack([upper, lower]).astype(jnp.bfloat16)

def reference(voltages, feed_position, beam_steering, synthesis_taps):
    delays = compute_delays(feed_position, beam_steering)
    frame_count = voltages.shape[1]
    width = math.gcd(C, 8)
    count = C // width

    def one_block(block_index):
        offset = block_index * width
        slab = lax.dynamic_slice_in_dim(voltages, offset, width, 3)
        channel_ids = offset + jnp.arange(width, dtype=jnp.int32)
        weights = make_weights(delays, channel_ids)
        product = jnp.einsum('stfc,cfk->stck', slab.astype(jnp.float32), weights.astype(jnp.float32))
        return combine(product)
    blocks = lax.map(one_block, jnp.arange(count, dtype=jnp.int32))
    beamed = jnp.transpose(blocks, (1, 2, 0, 3, 4)).reshape(2, frame_count, C, BEAMS)
    basis = make_basis()
    frames = jnp.einsum('stcb,scn->tbn', beamed.astype(jnp.float32), basis.astype(jnp.float32))
    frames = (frames * (1.0 / math.sqrt(C))).astype(jnp.bfloat16)
    leading = jnp.zeros((TAPS - 1,) + frames.shape[1:], jnp.bfloat16)
    extended = jnp.concatenate([leading, frames], axis=0).astype(jnp.float32)
    doubled = jnp.concatenate([synthesis_taps, synthesis_taps], axis=1)
    total = jnp.zeros(frames.shape, jnp.float32)
    for tap_index in range(TAPS):
        begin = TAPS - 1 - tap_index
        total = total + doubled[tap_index][None, None, :] * extended[begin:begin + frame_count]
    output = total.astype(jnp.bfloat16).reshape(frame_count, BEAMS, 2, C)
    return jnp.transpose(output, (2, 1, 0, 3))
```

```python
import functools
import math

import jax
import jax.numpy as jnp
from jax import lax
from jax.experimental import pallas as pl
from jax.experimental.pallas import tpu as pltpu
from jax.sharding import PartitionSpec as P

PHASES = 4096
ROWS = 32
DEPTH = 256


def passed_along(value, axis, steps):
    count = lax.axis_size(axis)
    initial, last = (max(0, -steps), min(count, count - steps))
    return lax.ppermute(value, axis, [(source, source + steps) for source in range(initial, last)])


def compute_delays(feed_position, beam_steering):
    first = feed_position[:, 0:1] * beam_steering[:, 0][None, :]
    second = feed_position[:, 1:2] * beam_steering[:, 1][None, :]
    return (first + second) % PHASES


def turn(steps, period):
    angles = (steps % period).astype(jnp.float32) * (2.0 * math.pi / period)
    return jnp.stack([jnp.cos(angles), jnp.sin(angles)])


def times(ar, ai, br, bi):
    return ar * br - ai * bi, ar * bi + ai * br


def beam_kernel(scale, v_ref, first_ref, unit_ref, out_ref, low_ref, high_ref, stride_ref, rounded_ref):
    width, rows, feeds = v_ref.shape
    half = rows // 2
    beams = first_ref.shape[2]
    bf16 = jnp.bfloat16

    @pl.when(pl.program_id(0) == 0)
    def _():
        @pl.loop(0, feeds // ROWS)
        def _(block):
            here = pl.ds(pl.multiple_of(block * ROWS, ROWS), ROWS)
            ur, ui = unit_ref[0, here, :], unit_ref[1, here, :]
            ar, ai = jnp.ones_like(ur), jnp.zeros_like(ui)
            for j in range(width):
                low_ref[j, 0, here, :] = ar.astype(bf16)
                low_ref[j, 1, here, :] = ai.astype(bf16)
                ar, ai = times(ar, ai, ur, ui)
            stride_ref[0, here, :] = ar
            stride_ref[1, here, :] = ai
            fr, fi = first_ref[0, here, :], first_ref[1, here, :]
            high_ref[0, here, :] = fr
            high_ref[1, here, :] = fi
            rounded_ref[0, here, :] = fr.astype(bf16)
            rounded_ref[1, here, :] = fi.astype(bf16)

    @pl.when(pl.program_id(0) > 0)
    def _():
        @pl.loop(0, feeds // ROWS)
        def _(block):
            here = pl.ds(pl.multiple_of(block * ROWS, ROWS), ROWS)
            hr, hi = times(high_ref[0, here, :], high_ref[1, here, :], stride_ref[0, here, :], stride_ref[1, here, :])
            high_ref[0, here, :] = hr
            high_ref[1, here, :] = hi
            rounded_ref[0, here, :] = hr.astype(bf16)
            rounded_ref[1, here, :] = hi.astype(bf16)

    for j in range(width):
        total = jnp.zeros((rows, 2 * beams), jnp.float32)
        for begin in range(0, feeds, DEPTH):
            here = slice(begin, begin + DEPTH)
            wr, wi = times(rounded_ref[0, here, :], rounded_ref[1, here, :], low_ref[j, 0, here, :], low_ref[j, 1, here, :])
            weights = jnp.concatenate([wr, wi], axis=1)
            total = total + jnp.dot(v_ref[j, :, here], weights, preferred_element_type=jnp.float32)
        upper, lower = total[:half], total[half:]
        real_part = upper[:, :beams] - lower[:, beams:]
        imag_part = upper[:, beams:] + lower[:, :beams]
        out_ref[j] = (jnp.concatenate([real_part, imag_part], axis=0) * scale).astype(bf16)


def beamform(turned, first, unit):
    chan_count, rows, feeds = turned.shape
    beams = first.shape[2]
    width = math.gcd(chan_count, 16)
    table = pl.BlockSpec((2, feeds, beams), lambda i: (0, 0, 0))
    return pl.pallas_call(
        functools.partial(beam_kernel, 1.0 / math.sqrt(feeds)),
        grid=(chan_count // width,),
        out_shape=jax.ShapeDtypeStruct((chan_count, rows, beams), jnp.bfloat16),
        in_specs=[pl.BlockSpec((width, rows, feeds), lambda i: (i, 0, 0)), table, table],
        out_specs=pl.BlockSpec((width, rows, beams), lambda i: (i, 0, 0)),
        scratch_shapes=[
            pltpu.VMEM((width, 2, feeds, beams), jnp.bfloat16),
            pltpu.VMEM((2, feeds, beams), jnp.float32),
            pltpu.VMEM((2, feeds, beams), jnp.float32),
            pltpu.VMEM((2, feeds, beams), jnp.bfloat16),
        ],
        compiler_params=pltpu.CompilerParams(vmem_limit_bytes=40 * 1024 * 1024),
    )(turned, first, unit)


def make_basis(size):
    width = math.gcd(size, 32)
    columns = lax.iota(jnp.int32, size)
    low = turn(lax.iota(jnp.int32, width)[:, None] * columns[None, :], size)
    high = turn(width * lax.iota(jnp.int32, size // width)[:, None] * columns[None, :], size)
    cosine, sine = times(high[0][:, None, :], high[1][:, None, :], low[0][None], low[1][None])
    cosine = cosine.reshape(size, size).astype(jnp.bfloat16)
    sine = sine.reshape(size, size).astype(jnp.bfloat16)
    upper = jnp.concatenate([cosine, sine], axis=1)
    lower = jnp.concatenate([-sine, cosine], axis=1)
    return jnp.stack([upper, lower])


def synthesize(beamed, basis):
    size = basis.shape[1]
    frames = jnp.einsum("bstc,scn->tbn", beamed, basis, preferred_element_type=jnp.float32)
    return (frames * (1.0 / math.sqrt(size))).astype(jnp.bfloat16)


def apply_taps(extended, synthesis_taps):
    taps, size = synthesis_taps.shape
    frame_count = extended.shape[0] - (taps - 1)
    widened = extended.astype(jnp.float32)
    doubled = jnp.concatenate([synthesis_taps, synthesis_taps], axis=1)
    total = jnp.zeros((frame_count,) + extended.shape[1:], jnp.float32)
    for tap_index in range(taps):
        begin = taps - 1 - tap_index
        total = total + doubled[tap_index][None, None, :] * widened[begin : begin + frame_count]
    output = total.astype(jnp.bfloat16).reshape(frame_count, extended.shape[1], 2, size)
    return jnp.transpose(output, (2, 1, 0, 3))


def on_device(voltages, feed_position, beam_steering, synthesis_taps):
    devices_chan = lax.axis_size("chan")
    size = voltages.shape[3]
    frame_count = voltages.shape[1]
    taps = synthesis_taps.shape[0]
    chan_count = size // devices_chan
    chan_start = lax.axis_index("chan") * chan_count
    delays = compute_delays(feed_position, beam_steering)
    first = turn(chan_start * delays, PHASES)
    unit = turn(delays, PHASES)
    turned = lax.all_to_all(voltages, "chan", split_axis=3, concat_axis=2, tiled=True)
    feeds = turned.shape[2]
    turned = jnp.transpose(turned.reshape(2 * frame_count, feeds, chan_count), (2, 0, 1))
    beamed = jnp.transpose(beamform(turned, first, unit), (2, 1, 0))
    regrouped = lax.all_to_all(beamed, "chan", split_axis=0, concat_axis=2, tiled=True)
    regrouped = regrouped.reshape(regrouped.shape[0], 2, frame_count, size)
    basis = make_basis(size)
    frames = synthesize(regrouped, basis)
    carried = passed_along(frames[frame_count - (taps - 1) :], "tm", 1)
    extended = jnp.concatenate([carried, frames], axis=0)
    return apply_taps(extended, synthesis_taps)


def solution(mesh):
    return jax.shard_map(
        on_device,
        mesh=mesh,
        in_specs=(P(None, ("group", "tm"), "chan", None), P(), P("group", None), P()),
        out_specs=P(None, "chan", ("group", "tm"), None),
        check_vma=False,
    )
```

```python
import functools
import math

import jax
import jax.numpy as jnp
from jax import lax
from jax.experimental import pallas as pl
from jax.experimental.pallas import tpu as pltpu
from jax.sharding import PartitionSpec as P

PHASES = 4096
ROWS = 32
CHUNKS = 4
WIDTH = 8


def passed_along(value, axis, steps):
    count = lax.axis_size(axis)
    initial, last = (max(0, -steps), min(count, count - steps))
    return lax.ppermute(value, axis, [(source, source + steps) for source in range(initial, last)])


def compute_delays(feed_position, beam_steering):
    first = feed_position[:, 0:1] * beam_steering[:, 0][None, :]
    second = feed_position[:, 1:2] * beam_steering[:, 1][None, :]
    return (first + second) % PHASES


def turn(steps, period):
    angles = (steps % period).astype(jnp.float32) * (2.0 * math.pi / period)
    return jnp.stack([jnp.cos(angles), jnp.sin(angles)])


def times(ar, ai, br, bi):
    return ar * br - ai * bi, ar * bi + ai * br


def beam_kernel(scale, v_ref, first_ref, unit_ref, out_ref, low_ref, high_ref, stride_ref, rounded_ref):
    sources, width, rows, depth = v_ref.shape
    feeds = sources * depth
    half = rows // 2
    beams = first_ref.shape[2]
    bf16 = jnp.bfloat16

    @pl.when(pl.program_id(0) == 0)
    def _():
        @pl.loop(0, feeds // ROWS)
        def _(block):
            here = pl.ds(pl.multiple_of(block * ROWS, ROWS), ROWS)
            ur, ui = unit_ref[0, here, :], unit_ref[1, here, :]
            ar, ai = jnp.ones_like(ur), jnp.zeros_like(ui)
            for j in range(width):
                low_ref[j, 0, here, :] = ar.astype(bf16)
                low_ref[j, 1, here, :] = ai.astype(bf16)
                ar, ai = times(ar, ai, ur, ui)
            stride_ref[0, here, :] = ar
            stride_ref[1, here, :] = ai
            fr, fi = first_ref[0, here, :], first_ref[1, here, :]
            high_ref[0, here, :] = fr
            high_ref[1, here, :] = fi
            rounded_ref[0, here, :] = fr.astype(bf16)
            rounded_ref[1, here, :] = fi.astype(bf16)

    @pl.when(pl.program_id(0) > 0)
    def _():
        @pl.loop(0, feeds // ROWS)
        def _(block):
            here = pl.ds(pl.multiple_of(block * ROWS, ROWS), ROWS)
            hr, hi = times(high_ref[0, here, :], high_ref[1, here, :], stride_ref[0, here, :], stride_ref[1, here, :])
            high_ref[0, here, :] = hr
            high_ref[1, here, :] = hi
            rounded_ref[0, here, :] = hr.astype(bf16)
            rounded_ref[1, here, :] = hi.astype(bf16)

    for j in range(width):
        total = jnp.zeros((rows, 2 * beams), jnp.float32)
        for source in range(sources):
            here = slice(source * depth, (source + 1) * depth)
            wr, wi = times(rounded_ref[0, here, :], rounded_ref[1, here, :], low_ref[j, 0, here, :], low_ref[j, 1, here, :])
            weights = jnp.concatenate([wr, wi], axis=1)
            total = total + jnp.dot(v_ref[source, j], weights, preferred_element_type=jnp.float32)
        upper, lower = total[:half], total[half:]
        real_part = upper[:, :beams] - lower[:, beams:]
        imag_part = upper[:, beams:] + lower[:, :beams]
        out_ref[j] = (jnp.concatenate([real_part, imag_part], axis=0) * scale).astype(bf16)


def beamform(turned, first, unit):
    sources, chan_count, rows, depth = turned.shape
    feeds = sources * depth
    beams = first.shape[2]
    width = math.gcd(chan_count, WIDTH)
    table = pl.BlockSpec((2, feeds, beams), lambda i: (0, 0, 0))
    return pl.pallas_call(
        functools.partial(beam_kernel, 1.0 / math.sqrt(feeds)),
        grid=(chan_count // width,),
        out_shape=jax.ShapeDtypeStruct((chan_count, rows, beams), jnp.bfloat16),
        in_specs=[pl.BlockSpec((sources, width, rows, depth), lambda i: (0, i, 0, 0)), table, table],
        out_specs=pl.BlockSpec((width, rows, beams), lambda i: (i, 0, 0)),
        scratch_shapes=[
            pltpu.VMEM((width, 2, feeds, beams), jnp.bfloat16),
            pltpu.VMEM((2, feeds, beams), jnp.float32),
            pltpu.VMEM((2, feeds, beams), jnp.float32),
            pltpu.VMEM((2, feeds, beams), jnp.bfloat16),
        ],
        cost_estimate=pl.CostEstimate(
            flops=8 * chan_count * rows * feeds * beams,
            bytes_accessed=2 * turned.size + 16 * feeds * beams,
            transcendentals=0,
        ),
        compiler_params=pltpu.CompilerParams(vmem_limit_bytes=40 * 1024 * 1024),
    )(turned, first, unit)


def make_basis(size):
    width = math.gcd(size, 32)
    columns = lax.iota(jnp.int32, size)
    low = turn(lax.iota(jnp.int32, width)[:, None] * columns[None, :], size)
    high = turn(width * lax.iota(jnp.int32, size // width)[:, None] * columns[None, :], size)
    cosine, sine = times(high[0][:, None, :], high[1][:, None, :], low[0][None], low[1][None])
    cosine = cosine.reshape(size, size).astype(jnp.bfloat16)
    sine = sine.reshape(size, size).astype(jnp.bfloat16)
    return jnp.concatenate([cosine, sine], axis=1)


def synthesize(beamed, basis):
    size = basis.shape[0]
    product = jnp.einsum("bstc,cn->stbn", beamed, basis, preferred_element_type=jnp.float32)
    real_part = product[0, ..., :size] - product[1, ..., size:]
    imag_part = product[0, ..., size:] + product[1, ..., :size]
    return (jnp.concatenate([real_part, imag_part], axis=-1) * (1.0 / math.sqrt(size))).astype(jnp.bfloat16)


def apply_taps(extended, synthesis_taps):
    taps, size = synthesis_taps.shape
    frame_count = extended.shape[0] - (taps - 1)
    widened = extended.astype(jnp.float32)
    doubled = jnp.concatenate([synthesis_taps, synthesis_taps], axis=1)
    total = jnp.zeros((frame_count,) + extended.shape[1:], jnp.float32)
    for tap_index in range(taps):
        begin = taps - 1 - tap_index
        total = total + doubled[tap_index][None, None, :] * widened[begin : begin + frame_count]
    output = total.astype(jnp.bfloat16).reshape(frame_count, extended.shape[1], 2, size)
    return jnp.transpose(output, (2, 1, 0, 3))


def on_device(voltages, feed_position, beam_steering, synthesis_taps):
    devices_chan = lax.axis_size("chan")
    size = voltages.shape[3]
    frame_count = voltages.shape[1]
    taps = synthesis_taps.shape[0]
    chan_count = size // devices_chan
    chan_start = lax.axis_index("chan") * chan_count
    delays = compute_delays(feed_position, beam_steering)
    unit = turn(delays, PHASES)
    feeds = voltages.shape[2]
    chunks = math.gcd(chan_count, CHUNKS)
    part = chan_count // chunks
    turned = jnp.transpose(voltages.reshape(2 * frame_count, feeds, size), (2, 0, 1))
    turned = lax.optimization_barrier(turned.reshape(devices_chan, chunks, part, 2 * frame_count, feeds))
    blocks = []
    for chunk in range(chunks):
        received = lax.all_to_all(turned[:, chunk], "chan", split_axis=0, concat_axis=0, tiled=True)
        first = turn((chan_start + chunk * part) * delays, PHASES)
        blocks.append(beamform(received, first, unit))
    beamed = jnp.transpose(jnp.concatenate(blocks, axis=0), (2, 1, 0))
    regrouped = lax.all_to_all(beamed, "chan", split_axis=0, concat_axis=2, tiled=True)
    regrouped = regrouped.reshape(regrouped.shape[0], 2, frame_count, size)
    basis = make_basis(size)
    frames = synthesize(regrouped, basis)
    carried = passed_along(frames[frame_count - (taps - 1) :], "tm", 1)
    extended = jnp.concatenate([carried, frames], axis=0)
    return apply_taps(extended, synthesis_taps)


def solution(mesh):
    return jax.shard_map(
        on_device,
        mesh=mesh,
        in_specs=(P(None, ("group", "tm"), "chan", None), P(), P("group", None), P()),
        out_specs=P(None, "chan", ("group", "tm"), None),
        check_vma=False,
    )
```

```python
import functools
import math

import jax
import jax.numpy as jnp
from jax import lax
from jax.experimental import pallas as pl
from jax.experimental.pallas import tpu as pltpu
from jax.sharding import PartitionSpec as P

PHASES = 4096
ROWS = 32
CHUNKS = 4
WIDTH = 8


def passed_along(value, axis, steps):
    count = lax.axis_size(axis)
    initial, last = (max(0, -steps), min(count, count - steps))
    return lax.ppermute(value, axis, [(source, source + steps) for source in range(initial, last)])


def compute_delays(feed_position, beam_steering):
    first = feed_position[:, 0:1] * beam_steering[:, 0][None, :]
    second = feed_position[:, 1:2] * beam_steering[:, 1][None, :]
    return (first + second) % PHASES


def turn(steps, period):
    angles = (steps % period).astype(jnp.float32) * (2.0 * math.pi / period)
    return jnp.stack([jnp.cos(angles), jnp.sin(angles)])


def times(ar, ai, br, bi):
    return ar * br - ai * bi, ar * bi + ai * br


def beam_kernel(scale, v_ref, first_ref, unit_ref, out_ref, low_ref, high_ref, stride_ref, rounded_ref):
    sources, width, rows, depth = v_ref.shape
    feeds = sources * depth
    half = rows // 2
    beams = first_ref.shape[2]
    bf16 = jnp.bfloat16

    @pl.when(pl.program_id(0) == 0)
    def _():
        @pl.loop(0, feeds // ROWS)
        def _(block):
            here = pl.ds(pl.multiple_of(block * ROWS, ROWS), ROWS)
            ur, ui = unit_ref[0, here, :], unit_ref[1, here, :]
            ar, ai = jnp.ones_like(ur), jnp.zeros_like(ui)
            for j in range(width):
                low_ref[j, 0, here, :] = ar.astype(bf16)
                low_ref[j, 1, here, :] = ai.astype(bf16)
                ar, ai = times(ar, ai, ur, ui)
            stride_ref[0, here, :] = ar
            stride_ref[1, here, :] = ai
            fr, fi = first_ref[0, here, :], first_ref[1, here, :]
            high_ref[0, here, :] = fr
            high_ref[1, here, :] = fi
            rounded_ref[0, here, :] = fr.astype(bf16)
            rounded_ref[1, here, :] = fi.astype(bf16)

    @pl.when(pl.program_id(0) > 0)
    def _():
        @pl.loop(0, feeds // ROWS)
        def _(block):
            here = pl.ds(pl.multiple_of(block * ROWS, ROWS), ROWS)
            hr, hi = times(high_ref[0, here, :], high_ref[1, here, :], stride_ref[0, here, :], stride_ref[1, here, :])
            high_ref[0, here, :] = hr
            high_ref[1, here, :] = hi
            rounded_ref[0, here, :] = hr.astype(bf16)
            rounded_ref[1, here, :] = hi.astype(bf16)

    for j in range(width):
        total = jnp.zeros((rows, 2 * beams), jnp.float32)
        for source in range(sources):
            here = slice(source * depth, (source + 1) * depth)
            wr, wi = times(rounded_ref[0, here, :], rounded_ref[1, here, :], low_ref[j, 0, here, :], low_ref[j, 1, here, :])
            weights = jnp.concatenate([wr, wi], axis=1)
            total = total + jnp.dot(v_ref[source, j], weights, preferred_element_type=jnp.float32)
        upper, lower = total[:half], total[half:]
        real_part = upper[:, :beams] - lower[:, beams:]
        imag_part = upper[:, beams:] + lower[:, :beams]
        out_ref[j] = (jnp.concatenate([real_part, imag_part], axis=0) * scale).astype(bf16)


def beamform(turned, first, unit):
    sources, chan_count, rows, depth = turned.shape
    feeds = sources * depth
    beams = first.shape[2]
    width = math.gcd(chan_count, WIDTH)
    table = pl.BlockSpec((2, feeds, beams), lambda i: (0, 0, 0))
    return pl.pallas_call(
        functools.partial(beam_kernel, 1.0 / math.sqrt(feeds)),
        grid=(chan_count // width,),
        out_shape=jax.ShapeDtypeStruct((chan_count, rows, beams), jnp.bfloat16),
        in_specs=[pl.BlockSpec((sources, width, rows, depth), lambda i: (0, i, 0, 0)), table, table],
        out_specs=pl.BlockSpec((width, rows, beams), lambda i: (i, 0, 0)),
        scratch_shapes=[
            pltpu.VMEM((width, 2, feeds, beams), jnp.bfloat16),
            pltpu.VMEM((2, feeds, beams), jnp.float32),
            pltpu.VMEM((2, feeds, beams), jnp.float32),
            pltpu.VMEM((2, feeds, beams), jnp.bfloat16),
        ],
        cost_estimate=pl.CostEstimate(
            flops=8 * chan_count * rows * feeds * beams,
            bytes_accessed=2 * turned.size + 16 * feeds * beams,
            transcendentals=0,
        ),
        compiler_params=pltpu.CompilerParams(vmem_limit_bytes=40 * 1024 * 1024),
    )(turned, first, unit)


def make_basis(size):
    width = math.gcd(size, 32)
    columns = lax.iota(jnp.int32, size)
    low = turn(lax.iota(jnp.int32, width)[:, None] * columns[None, :], size)
    high = turn(width * lax.iota(jnp.int32, size // width)[:, None] * columns[None, :], size)
    cosine, sine = times(high[0][:, None, :], high[1][:, None, :], low[0][None], low[1][None])
    cosine = cosine.reshape(size, size).astype(jnp.bfloat16)
    sine = sine.reshape(size, size).astype(jnp.bfloat16)
    return jnp.concatenate([cosine, sine], axis=1)


def synthesize(beamed, basis):
    size = basis.shape[0]
    product = jnp.einsum("bstc,cn->stbn", beamed, basis, preferred_element_type=jnp.float32)
    real_part = product[0, ..., :size] - product[1, ..., size:]
    imag_part = product[0, ..., size:] + product[1, ..., :size]
    return (jnp.concatenate([real_part, imag_part], axis=-1) * (1.0 / math.sqrt(size))).astype(jnp.bfloat16)


def apply_taps(extended, synthesis_taps):
    taps, size = synthesis_taps.shape
    frame_count = extended.shape[0] - (taps - 1)
    widened = extended.astype(jnp.float32)
    doubled = jnp.concatenate([synthesis_taps, synthesis_taps], axis=1)
    total = jnp.zeros((frame_count,) + extended.shape[1:], jnp.float32)
    for tap_index in range(taps):
        begin = taps - 1 - tap_index
        total = total + doubled[tap_index][None, None, :] * widened[begin : begin + frame_count]
    output = total.astype(jnp.bfloat16).reshape(frame_count, extended.shape[1], 2, size)
    return jnp.transpose(output, (2, 1, 0, 3))


def on_device(voltages, feed_position, beam_steering, synthesis_taps):
    devices_chan = lax.axis_size("chan")
    size = voltages.shape[3]
    frame_count = voltages.shape[1]
    taps = synthesis_taps.shape[0]
    chan_count = size // devices_chan
    chan_start = lax.axis_index("chan") * chan_count
    delays = compute_delays(feed_position, beam_steering)
    unit = turn(delays, PHASES)
    feeds = voltages.shape[2]
    chunks = math.gcd(chan_count, CHUNKS)
    part = chan_count // chunks
    turned = jnp.transpose(voltages.reshape(2 * frame_count, feeds, size), (2, 0, 1))
    turned = lax.optimization_barrier(turned.reshape(devices_chan, chunks, part, 2 * frame_count, feeds))
    first = turn(chan_start * delays, PHASES)
    stride, left = unit, part
    total = None
    while left:
        if left % 2:
            total = stride if total is None else jnp.stack(times(*total, *stride))
        left //= 2
        stride = jnp.stack(times(*stride, *stride))
    firsts = [first]
    for _ in range(1, chunks):
        firsts.append(jnp.stack(times(*firsts[-1], *total)))
    basis = make_basis(size)
    blocks = []
    for chunk in range(chunks):
        if chunk == 1:
            turned, unit, firsts = lax.optimization_barrier((turned, unit, firsts))
        if chunk == 2:
            turned, basis = lax.optimization_barrier((turned, basis))
        if chunk > 1:
            turned, blocks[chunk - 2] = lax.optimization_barrier((turned, blocks[chunk - 2]))
        if chunk > 0:
            received, start = blocks[chunk - 1]
            turned, received = lax.optimization_barrier((turned, received))
            blocks[chunk - 1] = (received, start)
        received = lax.all_to_all(turned[:, chunk], "chan", split_axis=0, concat_axis=0, tiled=True)
        blocks.append((received, firsts[chunk]))
        if chunk > 0:
            blocks[chunk - 1] = beamform(*blocks[chunk - 1], unit)
    blocks[-1] = beamform(*blocks[-1], unit)
    beamed = jnp.transpose(jnp.concatenate(blocks, axis=0), (2, 1, 0))
    regrouped = lax.all_to_all(beamed, "chan", split_axis=0, concat_axis=2, tiled=True)
    regrouped = regrouped.reshape(regrouped.shape[0], 2, frame_count, size)
    frames = synthesize(regrouped, basis)
    carried = passed_along(frames[frame_count - (taps - 1) :], "tm", 1)
    extended = jnp.concatenate([carried, frames], axis=0)
    return apply_taps(extended, synthesis_taps)


def solution(mesh):
    return jax.shard_map(
        on_device,
        mesh=mesh,
        in_specs=(P(None, ("group", "tm"), "chan", None), P(), P("group", None), P()),
        out_specs=P(None, "chan", ("group", "tm"), None),
        check_vma=False,
    )
```

```python
import functools
import math

import jax
import jax.numpy as jnp
from jax import lax
from jax.experimental import pallas as pl
from jax.experimental.pallas import tpu as pltpu
from jax.sharding import PartitionSpec as P

PHASES = 4096
ROWS = 32
CHUNKS = 2
WIDTH = 16


def passed_along(value, axis, steps):
    count = lax.axis_size(axis)
    initial, last = (max(0, -steps), min(count, count - steps))
    return lax.ppermute(value, axis, [(source, source + steps) for source in range(initial, last)])


def compute_delays(feed_position, beam_steering):
    first = feed_position[:, 0:1] * beam_steering[:, 0][None, :]
    second = feed_position[:, 1:2] * beam_steering[:, 1][None, :]
    return (first + second) % PHASES


def turn(steps, period):
    angles = (steps % period).astype(jnp.float32) * (2.0 * math.pi / period)
    return jnp.stack([jnp.cos(angles), jnp.sin(angles)])


def times(ar, ai, br, bi):
    return ar * br - ai * bi, ar * bi + ai * br


def beam_kernel(scale, v_ref, first_ref, unit_ref, out_ref, low_ref, high_ref, stride_ref, rounded_ref):
    sources, width, rows, depth = v_ref.shape
    feeds = sources * depth
    half = rows // 2
    beams = first_ref.shape[2]
    bf16 = jnp.bfloat16

    @pl.when(pl.program_id(0) == 0)
    def _():
        @pl.loop(0, feeds // ROWS)
        def _(block):
            here = pl.ds(pl.multiple_of(block * ROWS, ROWS), ROWS)
            ur, ui = unit_ref[0, here, :], unit_ref[1, here, :]
            ar, ai = jnp.ones_like(ur), jnp.zeros_like(ui)
            for j in range(width):
                low_ref[j, 0, here, :] = ar.astype(bf16)
                low_ref[j, 1, here, :] = ai.astype(bf16)
                ar, ai = times(ar, ai, ur, ui)
            stride_ref[0, here, :] = ar
            stride_ref[1, here, :] = ai
            fr, fi = first_ref[0, here, :], first_ref[1, here, :]
            high_ref[0, here, :] = fr
            high_ref[1, here, :] = fi
            rounded_ref[0, here, :] = fr.astype(bf16)
            rounded_ref[1, here, :] = fi.astype(bf16)

    @pl.when(pl.program_id(0) > 0)
    def _():
        @pl.loop(0, feeds // ROWS)
        def _(block):
            here = pl.ds(pl.multiple_of(block * ROWS, ROWS), ROWS)
            hr, hi = times(high_ref[0, here, :], high_ref[1, here, :], stride_ref[0, here, :], stride_ref[1, here, :])
            high_ref[0, here, :] = hr
            high_ref[1, here, :] = hi
            rounded_ref[0, here, :] = hr.astype(bf16)
            rounded_ref[1, here, :] = hi.astype(bf16)

    for j in range(width):
        total = jnp.zeros((rows, 2 * beams), jnp.float32)
        for source in range(sources):
            here = slice(source * depth, (source + 1) * depth)
            wr, wi = times(rounded_ref[0, here, :], rounded_ref[1, here, :], low_ref[j, 0, here, :], low_ref[j, 1, here, :])
            weights = jnp.concatenate([wr, wi], axis=1)
            total = total + jnp.dot(v_ref[source, j], weights, preferred_element_type=jnp.float32)
        upper, lower = total[:half], total[half:]
        real_part = upper[:, :beams] - lower[:, beams:]
        imag_part = upper[:, beams:] + lower[:, :beams]
        out_ref[j] = (jnp.concatenate([real_part, imag_part], axis=0) * scale).astype(bf16)


def beamform(turned, first, unit):
    sources, chan_count, rows, depth = turned.shape
    feeds = sources * depth
    beams = first.shape[2]
    width = math.gcd(chan_count, WIDTH)
    table = pl.BlockSpec((2, feeds, beams), lambda i: (0, 0, 0))
    return pl.pallas_call(
        functools.partial(beam_kernel, 1.0 / math.sqrt(feeds)),
        grid=(chan_count // width,),
        out_shape=jax.ShapeDtypeStruct((chan_count, rows, beams), jnp.bfloat16),
        in_specs=[pl.BlockSpec((sources, width, rows, depth), lambda i: (0, i, 0, 0)), table, table],
        out_specs=pl.BlockSpec((width, rows, beams), lambda i: (i, 0, 0)),
        scratch_shapes=[
            pltpu.VMEM((width, 2, feeds, beams), jnp.bfloat16),
            pltpu.VMEM((2, feeds, beams), jnp.float32),
            pltpu.VMEM((2, feeds, beams), jnp.float32),
            pltpu.VMEM((2, feeds, beams), jnp.bfloat16),
        ],
        cost_estimate=pl.CostEstimate(
            flops=8 * chan_count * rows * feeds * beams,
            bytes_accessed=2 * turned.size + 16 * feeds * beams,
            transcendentals=0,
        ),
        compiler_params=pltpu.CompilerParams(vmem_limit_bytes=40 * 1024 * 1024),
    )(turned, first, unit)


def make_basis(size):
    width = math.gcd(size, 32)
    columns = lax.iota(jnp.int32, size)
    low = turn(lax.iota(jnp.int32, width)[:, None] * columns[None, :], size)
    high = turn(width * lax.iota(jnp.int32, size // width)[:, None] * columns[None, :], size)
    cosine, sine = times(high[0][:, None, :], high[1][:, None, :], low[0][None], low[1][None])
    cosine = cosine.reshape(size, size).astype(jnp.bfloat16)
    sine = sine.reshape(size, size).astype(jnp.bfloat16)
    return jnp.concatenate([cosine, sine], axis=1)


def synthesize(beamed, basis):
    size = basis.shape[0]
    product = jnp.einsum("bstc,cn->stbn", beamed, basis, preferred_element_type=jnp.float32)
    real_part = product[0, ..., :size] - product[1, ..., size:]
    imag_part = product[0, ..., size:] + product[1, ..., :size]
    return (jnp.concatenate([real_part, imag_part], axis=-1) * (1.0 / math.sqrt(size))).astype(jnp.bfloat16)


def apply_taps(extended, synthesis_taps):
    taps, size = synthesis_taps.shape
    frame_count = extended.shape[0] - (taps - 1)
    widened = extended.astype(jnp.float32)
    doubled = jnp.concatenate([synthesis_taps, synthesis_taps], axis=1)
    total = jnp.zeros((frame_count,) + extended.shape[1:], jnp.float32)
    for tap_index in range(taps):
        begin = taps - 1 - tap_index
        total = total + doubled[tap_index][None, None, :] * widened[begin : begin + frame_count]
    output = total.astype(jnp.bfloat16).reshape(frame_count, extended.shape[1], 2, size)
    return jnp.transpose(output, (2, 1, 0, 3))


def on_device(voltages, feed_position, beam_steering, synthesis_taps):
    devices_chan = lax.axis_size("chan")
    size = voltages.shape[3]
    frame_count = voltages.shape[1]
    taps = synthesis_taps.shape[0]
    chan_count = size // devices_chan
    chan_start = lax.axis_index("chan") * chan_count
    delays = compute_delays(feed_position, beam_steering)
    unit = turn(delays, PHASES)
    feeds = voltages.shape[2]
    chunks = math.gcd(chan_count, CHUNKS)
    part = chan_count // chunks
    turned = jnp.transpose(voltages.reshape(2 * frame_count, feeds, size), (2, 0, 1))
    turned = lax.optimization_barrier(turned.reshape(devices_chan, chunks, part, 2 * frame_count, feeds))
    first = turn(chan_start * delays, PHASES)
    stride, left = unit, part
    total = None
    while left:
        if left % 2:
            total = stride if total is None else jnp.stack(times(*total, *stride))
        left //= 2
        stride = jnp.stack(times(*stride, *stride))
    firsts = [first]
    for _ in range(1, chunks):
        firsts.append(jnp.stack(times(*firsts[-1], *total)))
    basis = make_basis(size)
    blocks = []
    for chunk in range(chunks):
        if chunk == 1:
            turned, unit, firsts = lax.optimization_barrier((turned, unit, firsts))
        if chunk == 2:
            turned, basis = lax.optimization_barrier((turned, basis))
        if chunk > 1:
            turned, blocks[chunk - 2] = lax.optimization_barrier((turned, blocks[chunk - 2]))
        if chunk > 0:
            received, start = blocks[chunk - 1]
            turned, received = lax.optimization_barrier((turned, received))
            blocks[chunk - 1] = (received, start)
        received = lax.all_to_all(turned[:, chunk], "chan", split_axis=0, concat_axis=0, tiled=True)
        blocks.append((received, firsts[chunk]))
        if chunk > 0:
            blocks[chunk - 1] = beamform(*blocks[chunk - 1], unit)
    blocks[-1] = beamform(*blocks[-1], unit)
    beamed = jnp.transpose(jnp.concatenate(blocks, axis=0), (2, 1, 0))
    regrouped = lax.all_to_all(beamed, "chan", split_axis=0, concat_axis=2, tiled=True)
    regrouped = regrouped.reshape(regrouped.shape[0], 2, frame_count, size)
    frames = synthesize(regrouped, basis)
    carried = passed_along(frames[frame_count - (taps - 1) :], "tm", 1)
    extended = jnp.concatenate([carried, frames], axis=0)
    return apply_taps(extended, synthesis_taps)


def solution(mesh):
    return jax.shard_map(
        on_device,
        mesh=mesh,
        in_specs=(P(None, ("group", "tm"), "chan", None), P(), P("group", None), P()),
        out_specs=P(None, "chan", ("group", "tm"), None),
        check_vma=False,
    )
```

```python
import functools
import math

import jax
import jax.numpy as jnp
from jax import lax
from jax.experimental import pallas as pl
from jax.experimental.pallas import tpu as pltpu
from jax.sharding import PartitionSpec as P

PHASES = 4096
ROWS = 32
CHUNKS = 2
WIDTH = 16


def passed_along(value, axis, steps):
    count = lax.axis_size(axis)
    initial, last = (max(0, -steps), min(count, count - steps))
    return lax.ppermute(value, axis, [(source, source + steps) for source in range(initial, last)])


def compute_delays(feed_position, beam_steering):
    first = feed_position[:, 0:1] * beam_steering[:, 0][None, :]
    second = feed_position[:, 1:2] * beam_steering[:, 1][None, :]
    return (first + second) % PHASES


def turn(steps, period):
    angles = (steps % period).astype(jnp.float32) * (2.0 * math.pi / period)
    return jnp.stack([jnp.cos(angles), jnp.sin(angles)])


def times(ar, ai, br, bi):
    return ar * br - ai * bi, ar * bi + ai * br


def beam_kernel(scale, v_ref, first_ref, unit_ref, out_ref, low_ref, high_ref, stride_ref, rounded_ref):
    sources, width, rows, depth = v_ref.shape
    feeds = sources * depth
    half = rows // 2
    beams = first_ref.shape[2]
    bf16 = jnp.bfloat16

    @pl.when(pl.program_id(0) == 0)
    def _():
        @pl.loop(0, feeds // ROWS)
        def _(block):
            here = pl.ds(pl.multiple_of(block * ROWS, ROWS), ROWS)
            ur, ui = unit_ref[0, here, :], unit_ref[1, here, :]
            ar, ai = jnp.ones_like(ur), jnp.zeros_like(ui)
            for j in range(width):
                low_ref[j, 0, here, :] = ar.astype(bf16)
                low_ref[j, 1, here, :] = ai.astype(bf16)
                ar, ai = times(ar, ai, ur, ui)
            stride_ref[0, here, :] = ar
            stride_ref[1, here, :] = ai
            fr, fi = first_ref[0, here, :], first_ref[1, here, :]
            high_ref[0, here, :] = fr
            high_ref[1, here, :] = fi
            rounded_ref[0, here, :] = fr.astype(bf16)
            rounded_ref[1, here, :] = fi.astype(bf16)

    @pl.when(pl.program_id(0) > 0)
    def _():
        @pl.loop(0, feeds // ROWS)
        def _(block):
            here = pl.ds(pl.multiple_of(block * ROWS, ROWS), ROWS)
            hr, hi = times(high_ref[0, here, :], high_ref[1, here, :], stride_ref[0, here, :], stride_ref[1, here, :])
            high_ref[0, here, :] = hr
            high_ref[1, here, :] = hi
            rounded_ref[0, here, :] = hr.astype(bf16)
            rounded_ref[1, here, :] = hi.astype(bf16)

    for j in range(width):
        total = jnp.zeros((rows, 2 * beams), jnp.float32)
        for source in range(sources):
            here = slice(source * depth, (source + 1) * depth)
            wr, wi = times(rounded_ref[0, here, :], rounded_ref[1, here, :], low_ref[j, 0, here, :], low_ref[j, 1, here, :])
            weights = jnp.concatenate([wr, wi], axis=1)
            total = total + jnp.dot(v_ref[source, j], weights, preferred_element_type=jnp.float32)
        upper, lower = total[:half], total[half:]
        real_part = upper[:, :beams] - lower[:, beams:]
        imag_part = upper[:, beams:] + lower[:, :beams]
        out_ref[j] = (jnp.concatenate([real_part, imag_part], axis=0) * scale).astype(bf16)


def beamform(turned, first, unit):
    sources, chan_count, rows, depth = turned.shape
    feeds = sources * depth
    beams = first.shape[2]
    width = math.gcd(chan_count, WIDTH)
    table = pl.BlockSpec((2, feeds, beams), lambda i: (0, 0, 0))
    return pl.pallas_call(
        functools.partial(beam_kernel, 1.0 / math.sqrt(feeds)),
        grid=(chan_count // width,),
        out_shape=jax.ShapeDtypeStruct((chan_count, rows, beams), jnp.bfloat16),
        in_specs=[pl.BlockSpec((sources, width, rows, depth), lambda i: (0, i, 0, 0)), table, table],
        out_specs=pl.BlockSpec((width, rows, beams), lambda i: (i, 0, 0)),
        scratch_shapes=[
            pltpu.VMEM((width, 2, feeds, beams), jnp.bfloat16),
            pltpu.VMEM((2, feeds, beams), jnp.float32),
            pltpu.VMEM((2, feeds, beams), jnp.float32),
            pltpu.VMEM((2, feeds, beams), jnp.bfloat16),
        ],
        cost_estimate=pl.CostEstimate(
            flops=8 * chan_count * rows * feeds * beams,
            bytes_accessed=2 * turned.size + 16 * feeds * beams,
            transcendentals=0,
        ),
        compiler_params=pltpu.CompilerParams(vmem_limit_bytes=40 * 1024 * 1024),
    )(turned, first, unit)


def make_basis(size):
    width = math.gcd(size, 32)
    columns = lax.iota(jnp.int32, size)
    low = turn(lax.iota(jnp.int32, width)[:, None] * columns[None, :], size)
    high = turn(width * lax.iota(jnp.int32, size // width)[:, None] * columns[None, :], size)
    cosine, sine = times(high[0][:, None, :], high[1][:, None, :], low[0][None], low[1][None])
    cosine = cosine.reshape(size, size).astype(jnp.bfloat16)
    sine = sine.reshape(size, size).astype(jnp.bfloat16)
    return jnp.concatenate([cosine, sine], axis=1)


def synthesize(beamed, basis):
    size = basis.shape[0]
    product = jnp.einsum("bstc,cn->stbn", beamed, basis, preferred_element_type=jnp.float32)
    real_part = product[0, ..., :size] - product[1, ..., size:]
    imag_part = product[0, ..., size:] + product[1, ..., :size]
    return (jnp.concatenate([real_part, imag_part], axis=-1) * (1.0 / math.sqrt(size))).astype(jnp.bfloat16)


def apply_taps(extended, synthesis_taps):
    taps, size = synthesis_taps.shape
    frame_count = extended.shape[0] - (taps - 1)
    widened = extended.astype(jnp.float32)
    doubled = jnp.concatenate([synthesis_taps, synthesis_taps], axis=1)
    total = jnp.zeros((frame_count,) + extended.shape[1:], jnp.float32)
    for tap_index in range(taps):
        begin = taps - 1 - tap_index
        total = total + doubled[tap_index][None, None, :] * widened[begin : begin + frame_count]
    output = total.astype(jnp.bfloat16).reshape(frame_count, extended.shape[1], 2, size)
    return jnp.transpose(output, (2, 1, 0, 3))


def on_device(voltages, feed_position, beam_steering, synthesis_taps):
    devices_chan = lax.axis_size("chan")
    size = voltages.shape[3]
    frame_count = voltages.shape[1]
    taps = synthesis_taps.shape[0]
    chan_count = size // devices_chan
    chan_start = lax.axis_index("chan") * chan_count
    delays = compute_delays(feed_position, beam_steering)
    unit = turn(delays, PHASES)
    feeds = voltages.shape[2]
    chunks = math.gcd(chan_count, CHUNKS)
    part = chan_count // chunks
    turned = jnp.transpose(voltages.reshape(2 * frame_count, feeds, size), (2, 0, 1))
    turned = lax.optimization_barrier(turned.reshape(devices_chan, chunks, part, 2 * frame_count, feeds))
    first = turn(chan_start * delays, PHASES)
    stride, left = unit, part
    total = None
    while left:
        if left % 2:
            total = stride if total is None else jnp.stack(times(*total, *stride))
        left //= 2
        stride = jnp.stack(times(*stride, *stride))
    firsts = [first]
    for _ in range(1, chunks):
        firsts.append(jnp.stack(times(*firsts[-1], *total)))
    basis = make_basis(size)
    blocks = []
    for chunk in range(chunks):
        if chunk == 1:
            turned, unit, firsts, basis = lax.optimization_barrier((turned, unit, firsts, basis))
        if chunk > 1:
            turned, blocks[chunk - 2] = lax.optimization_barrier((turned, blocks[chunk - 2]))
        piece = turned[:, chunk]
        if chunk > 0:
            received, start = blocks[chunk - 1]
            piece, received = lax.optimization_barrier((piece, received))
            blocks[chunk - 1] = (received, start)
        received = lax.all_to_all(piece, "chan", split_axis=0, concat_axis=0, tiled=True)
        blocks.append((received, firsts[chunk]))
        if chunk > 0:
            blocks[chunk - 1] = beamform(*blocks[chunk - 1], unit)
    blocks[-1] = beamform(*blocks[-1], unit)
    beamed = jnp.transpose(jnp.concatenate(blocks, axis=0), (2, 1, 0))
    regrouped = lax.all_to_all(beamed, "chan", split_axis=0, concat_axis=2, tiled=True)
    regrouped = regrouped.reshape(regrouped.shape[0], 2, frame_count, size)
    frames = synthesize(regrouped, basis)
    carried = passed_along(frames[frame_count - (taps - 1) :], "tm", 1)
    extended = jnp.concatenate([carried, frames], axis=0)
    return apply_taps(extended, synthesis_taps)


def solution(mesh):
    return jax.shard_map(
        on_device,
        mesh=mesh,
        in_specs=(P(None, ("group", "tm"), "chan", None), P(), P("group", None), P()),
        out_specs=P(None, "chan", ("group", "tm"), None),
        check_vma=False,
    )
```
